32 devices in a mesh: groups: 2 (over y), expert: 8 (over z, core), tensor: 2 (over x), dp: 1.
Axes of the slice: x: 2, y: 2, z: 4, core: 2. Of those that a mesh axis runs over, the one named last changes fastest.
Arguments:
- tokens: bfloat16 [2, 512, 4096], P(None, ('groups', 'expert', 'dp'), 'tensor'), parts along dimension 1, may hold values from -6 to 6
- expert_ids: int32 [2, 512, 16], P(None, ('groups', 'expert', 'dp')), parts along dimension 1, may hold values from 0 to 31, all different within a row; in each aligned block of 32 rows (0 to 31, 32 to 63, ..., all dimensions but the last counted through in order) at most 32 rows name the same one
- route_weights: int32 [2, 512, 16], P(None, ('groups', 'expert', 'dp')), parts along dimension 1, may hold values from 1 to 255
- expert_slot: int32 [32], replicated, may hold values from 0 to 31, each once
- latent_down: bfloat16 [4096, 1024], P('tensor'), may hold values from -0.09375 to 0.09375
- gate_proj: bfloat16 [32, 1024, 1024], P('expert', None, 'tensor'), may hold values from -0.1875 to 0.1875
- up_proj: bfloat16 [32, 1024, 1024], P('expert', None, 'tensor'), may hold values from -0.1875 to 0.1875
- down_proj: bfloat16 [32, 1024, 1024], P('expert', 'tensor'), may hold values from -0.1875 to 0.1875
- latent_up: bfloat16 [1024, 4096], P('tensor'), may hold values from -1.5 to 1.5
Outputs:
- layer_out: bfloat16 [2, 512, 4096], P(None, ('groups', 'expert', 'dp'), 'tensor'), parts along dimension 1
The draws below stay inside these ranges and needn't reach their ends.
There are 2 independent parts, one for each index of `groups`. The reference program is written for one: setup_inputs(seed, part) draws one part's arguments, and reference() takes and returns one part's arrays. A program takes and returns all parts, laid end to end along the dimension named above; an argument that names none is the same for every part. Nothing has to cross between parts.
Inputs may be any that keep to these rules, and one draw needn't show every extreme that they name: `expert_ids`: each row names 16 different experts. In each aligned block of 32 rows (the rows of one device in one batch) no expert is named by more than 32 rows, and in some block one expert is named by exactly 32 rows. `expert_slot`: A permutation: every slot serves exactly one expert.
All inputs are finite; a program needn't handle non-finite values.
Results may differ from the reference program's by a relative error of at most 0.029.
Values may be sent and summed in bfloat16 or wider, within the bound.
No kernel may reach another device: no remote copies, remote signals or barrier semaphores. Data moves between devices by JAX's collectives and lax.ppermute only.
A program may use at most 64 MiB of HBM per device.

```python
import math
import jax
import jax.numpy as jnp
import numpy as np
from jax import lax

D = 4096
L = 1024
H = 1024
TOPK = 16
EXP_DEV = 4
STEPS = 2
TOK_DEV = 32
EXPERTS = 32
TOKENS = 256
CAP = 32
N_EXPERT = 8
N_TENSOR = 2


def touch_ends(values, rng, low, top_value):
    longest = values.shape.index(max(values.shape))
    spots = []
    for shift in (0, 1):
        where = [jax.random.randint(jax.random.fold_in(rng, axis), (), 0, length) for axis, length in enumerate(values.shape)]
        where[longest] = (where[longest] + shift) % values.shape[longest]
        spots.append(tuple(where))
    return values.at[spots[0]].set(low).at[spots[1]].set(top_value)


def shard_levels(own_key, extent, cuts, low, largest):
    gain = 1.0
    for axis_at, parts in cuts:
        heights = jax.random.uniform(jax.random.fold_in(jax.random.fold_in(own_key, 6), axis_at), (parts,), jnp.float32, low / len(cuts), largest / len(cuts))
        gain = gain * jnp.repeat(jnp.exp(heights), extent[axis_at] // parts).reshape((-1,) + (1,) * (len(extent) - 1 - axis_at))
    return gain


def deal_out(key, own, number, rows, amount, top, reach, slope):
    sequence = jax.random.permutation(key, amount)
    heavy_load, usual = portions_of(amount, rows * top, reach, slope, True), portions_of(amount, rows * top, reach, slope, False)
    places = jnp.arange(amount)

    def named(tallies, rotation):
        used = int((tallies > 0).sum())
        fixed = max(1, used // 4)
        moved = fixed + (places - fixed + rotation * (used - fixed)) % max(1, amount - fixed)
        return jnp.zeros((amount,), jnp.int32).at[sequence[jnp.where(places < fixed, places, moved)]].set(jnp.asarray(tallies, jnp.int32))

    tallies = jnp.where(number % 4 == 0, named(heavy_load, number // 4), named(usual, number - number // 4 - 1))
    mixed = jax.random.permutation(jax.random.fold_in(own, 3), amount)
    donor, receiver = mixed[0:amount // 2 * 2:2], mixed[1:amount // 2 * 2:2]
    margin = jnp.minimum(tallies[donor] - 1, reach - tallies[receiver]) // 2
    margin = jnp.where((donor == sequence[0]) | (receiver == sequence[0]) | (tallies[receiver] == 0), 0, jnp.maximum(margin, 0))
    moved = jax.random.randint(jax.random.fold_in(own, 4), (amount // 2,), 0, 1 << 20) % (margin + 1)
    tallies = tallies.at[donor].add(-moved).at[receiver].add(moved)
    members = jnp.searchsorted(jnp.cumsum(tallies), jnp.arange(rows * top), side="right").astype(jnp.int32)
    grid = members.reshape(top, rows).T
    grid = grid[jax.random.permutation(jax.random.fold_in(own, 1), rows)]
    rotation = jax.random.randint(jax.random.fold_in(own, 2), (rows, 1), 0, top)
    return jnp.take_along_axis(grid, (jnp.arange(top)[None, :] + rotation) % top, axis=1)


def portions_of(count, total, limit, slope, full):
    portions = [(1 << 20) // math.isqrt(standing ** slope) + 1 for standing in range(1, count + 1)]
    largest = limit if full else min(limit, max(-(-total // count), total * portions[0] // sum(portions)))
    least = 1 if total - largest >= count - 1 else 0
    counts, rest = [largest] + [least] * (count - 1), total - largest - least * (count - 1)
    while rest > 0:
        free = [i for i in range(1, count) if counts[i] < largest] or [i for i in range(1, count) if counts[i] < limit]
        pool, budget = sum([portions[i] for i in free]), rest
        for i in free:
            extra = min(limit - counts[i], max(1, budget * portions[i] // pool), rest)
            counts[i] = counts[i] + extra
            rest = rest - extra
    return np.array(counts)


def scatter_about(stream_key, shape, scale, reach, split=(), held_as=jnp.bfloat16):
    factor_of = shard_levels(stream_key, shape, split, -0.22, 0.18) if split else 1.0
    result = jax.random.normal(stream_key, shape, jnp.float32) * scale * factor_of
    return jnp.minimum(jnp.maximum(result, -reach), reach).astype(held_as)


def setup_inputs(seed: int = 0, part: int = 0) -> dict:
    keys = jax.random.split(jax.random.key(seed), 10)
    own_keys = jax.random.split(jax.random.fold_in(keys[9], part), 10)
    tokens = scatter_about(own_keys[0], (STEPS, TOKENS, D), 1.0, 6.0, ((1, 8), (2, 2)))
    expert_ids_keys = jax.random.split(jax.random.fold_in(own_keys[1], 1), STEPS * TOKENS // TOK_DEV)
    expert_ids_turns = jax.random.permutation(jax.random.fold_in(own_keys[1], 3), STEPS * TOKENS // TOK_DEV)
    expert_ids = jax.vmap(lambda own, number: deal_out(jax.random.fold_in(own_keys[1], 2), own, number, TOK_DEV, EXPERTS, TOPK, CAP, 1))(expert_ids_keys, expert_ids_turns).reshape((STEPS, TOKENS, TOPK))
    route_weights = touch_ends(jax.random.randint(own_keys[2], (STEPS, TOKENS, TOPK), 1, 256), jax.random.fold_in(own_keys[2], 1), 1, 255).astype(jnp.int32)
    expert_slot = jax.random.permutation(keys[3], EXPERTS).astype(jnp.int32)
    latent_down = scatter_about(keys[4], (D, L), D ** -0.5, 0.09375, ((0, 2),))
    gate_proj = scatter_about(keys[5], (EXPERTS, L, H), L ** -0.5, 0.1875, ((0, 8), (2, 2)))
    up_proj = scatter_about(keys[6], (EXPERTS, L, H), L ** -0.5, 0.1875, ((0, 8), (2, 2)))
    down_proj = scatter_about(keys[7], (EXPERTS, H, L), H ** -0.5, 0.1875, ((0, 8), (1, 2)))
    latent_up = scatter_about(keys[8], (L, D), (max(L // 64, 1)) ** -0.5, 1.5, ((0, 2),))
    return {"tokens": tokens, "expert_ids": expert_ids, "route_weights": route_weights, "expert_slot": expert_slot, "latent_down": latent_down, "gate_proj": gate_proj, "up_proj": up_proj, "down_proj": down_proj, "latent_up": latent_up}


def expert_rows(latent, rows_of, filled, gate_w, up_w, down_w):
    picked = jnp.where(filled[:, None], jnp.take(latent, rows_of, axis=0), jnp.zeros((), jnp.bfloat16))
    gate_act = jnp.dot(picked, gate_w, preferred_element_type=jnp.float32)
    up_act = jnp.dot(picked, up_w, preferred_element_type=jnp.float32)
    hidden = (jax.nn.silu(gate_act) * up_act).astype(jnp.bfloat16)
    slot_rows = hidden.shape[0]
    hid_blocks = hidden.reshape(slot_rows, N_TENSOR, H // N_TENSOR).astype(jnp.float32)
    down_blocks = down_w.reshape(N_TENSOR, H // N_TENSOR, L).astype(jnp.float32)
    partial_value = jnp.einsum("rnh,nhl->nrl", hid_blocks, down_blocks, precision=lax.Precision.HIGHEST)
    partial_value = partial_value.astype(jnp.bfloat16).astype(jnp.float32)
    return jnp.sum(partial_value, axis=0).astype(jnp.bfloat16)


def one_batch(inputs, chosen, weights, expert_slot, latent_down, gate_proj, up_proj, down_proj, latent_up):
    block_count = TOKENS // TOK_DEV
    slot_rows = block_count * CAP
    pair_count = TOKENS * TOPK
    weight_vals = weights.astype(jnp.float32)
    gates = weight_vals / jnp.sum(weight_vals, axis=1, keepdims=True)
    latent = jnp.dot(inputs, latent_down, preferred_element_type=jnp.float32).astype(jnp.bfloat16)
    slot_ids = expert_slot[chosen].astype(jnp.int32)
    flat_slots = slot_ids.reshape(pair_count)
    onehot = (flat_slots[:, None] == jnp.arange(EXPERTS, dtype=jnp.int32)[None, :]).astype(jnp.int32)
    position = jnp.sum(onehot * (jnp.cumsum(onehot, axis=0) - 1), axis=1).astype(jnp.int32)
    target = (flat_slots * slot_rows + position).astype(jnp.int32)
    source = jnp.full((EXPERTS * slot_rows,), -1, jnp.int32).at[target].set(jnp.arange(pair_count, dtype=jnp.int32))
    filled = source >= 0
    rows_of = jnp.where(filled, source // TOPK, 0).astype(jnp.int32)

    def per_slot(items):
        return expert_rows(latent, items[0], items[1], items[2], items[3], items[4])

    buffers = lax.map(per_slot, (rows_of.reshape(EXPERTS, slot_rows), filled.reshape(EXPERTS, slot_rows), gate_proj, up_proj, down_proj))
    expert_out = buffers.reshape(EXPERTS * slot_rows, L)[target].reshape(TOKENS, TOPK, L)
    owner = slot_ids // EXP_DEV
    grouping = (owner[:, :, None] == jnp.arange(N_EXPERT, dtype=jnp.int32)[None, None, :]).astype(jnp.float32) * gates[:, :, None]
    share = jnp.einsum("tkp,tkl->tpl", grouping, expert_out.astype(jnp.float32), precision=lax.Precision.HIGHEST).astype(jnp.bfloat16)
    mixed_rows = jnp.sum(share.astype(jnp.float32), axis=1).astype(jnp.bfloat16)
    projected = jnp.dot(mixed_rows, latent_up, preferred_element_type=jnp.float32)
    return (inputs.astype(jnp.float32) + projected).astype(jnp.bfloat16)


def reference(tokens, expert_ids, route_weights, expert_slot, latent_down, gate_proj, up_proj, down_proj, latent_up):
    results = []
    for step_index in range(STEPS):
        results.append(one_batch(tokens[step_index], expert_ids[step_index], route_weights[step_index], expert_slot, latent_down, gate_proj, up_proj, down_proj, latent_up))
    return jnp.stack(results)
```

```python
import functools

import jax
import jax.numpy as jnp
from jax import lax
from jax.experimental import pallas as pl
from jax.experimental.pallas import tpu as pltpu
from jax.sharding import PartitionSpec as P

LANES = 128


def expert_kernel(rows_ref, weight_ref, gate_ref, up_ref, down_ref, out_ref, total_ref):
    step = pl.program_id(0)

    @pl.when(step == 0)
    def _():
        total_ref[...] = jnp.zeros_like(total_ref)

    rows = rows_ref[...]
    gate_act = jnp.dot(rows, gate_ref[0], preferred_element_type=jnp.float32)
    up_act = jnp.dot(rows, up_ref[0], preferred_element_type=jnp.float32)
    lanes = lax.broadcasted_iota(jnp.int32, weight_ref.shape, 1)
    weight = jnp.sum(
        jnp.where(lanes == step, weight_ref[...], 0.0), axis=1, keepdims=True
    )
    hidden = (gate_act / (1.0 + jnp.exp(-gate_act)) * up_act * weight).astype(jnp.bfloat16)
    total_ref[...] += jnp.dot(hidden, down_ref[0], preferred_element_type=jnp.float32)

    @pl.when(step == pl.num_programs(0) - 1)
    def _():
        out_ref[...] = total_ref[...].astype(out_ref.dtype)


def experts(rows, weights, gate_proj, up_proj, down_proj):
    row_count, width = rows.shape
    local_count, _, hidden = gate_proj.shape
    return pl.pallas_call(
        expert_kernel,
        grid=(local_count,),
        in_specs=[
            pl.BlockSpec((row_count, width), lambda j: (0, 0)),
            pl.BlockSpec((row_count, LANES), lambda j: (0, 0)),
            pl.BlockSpec((1, width, hidden), lambda j: (j, 0, 0)),
            pl.BlockSpec((1, width, hidden), lambda j: (j, 0, 0)),
            pl.BlockSpec((1, hidden, width), lambda j: (j, 0, 0)),
        ],
        out_specs=pl.BlockSpec((row_count, width), lambda j: (0, 0)),
        out_shape=jax.ShapeDtypeStruct((row_count, width), jnp.bfloat16),
        scratch_shapes=[pltpu.VMEM((row_count, width), jnp.float32)],
        compiler_params=pltpu.CompilerParams(vmem_limit_bytes=40 * 1024 * 1024),
    )(rows, weights, gate_proj, up_proj, down_proj)


def shift(x, axis, size, by):
    return lax.ppermute(x, axis, [(i, (i + by) % size) for i in range(size)])


def add(*terms):
    return functools.reduce(jnp.add, [t.astype(jnp.float32) for t in terms])


def slot_weights(expert_ids, route_weights, expert_slot):
    expert_count = expert_slot.shape[0]
    every = jnp.arange(expert_count, dtype=jnp.int32)
    chosen = expert_ids[:, :, None] == every[None, None, :]
    by_expert = jnp.sum(jnp.where(chosen, route_weights[:, :, None], 0), axis=1)
    move = expert_slot[:, None] == every[None, :]
    by_slot = jnp.dot(
        by_expert.astype(jnp.bfloat16), move.astype(jnp.bfloat16), preferred_element_type=jnp.float32
    )
    return by_slot.astype(jnp.bfloat16)


def shards(
    tokens,
    expert_ids,
    route_weights,
    expert_slot,
    latent_down,
    gate_proj,
    up_proj,
    down_proj,
    latent_up,
):
    steps, step_rows, features = tokens.shape
    rows = steps * step_rows
    latent_width = latent_down.shape[1]
    local_count = gate_proj.shape[0]
    tensor_count = lax.axis_size("tensor")
    expert_axis = lax.axis_size("expert")
    pair = 2 if expert_axis % 2 == 0 else 1
    far = expert_axis // pair
    tensor_index = lax.axis_index("tensor")
    expert_index = lax.axis_index("expert")

    def swap(x):
        return lax.ppermute(x, "expert", [(i, i ^ 1) for i in range(expert_axis)])

    inputs = tokens.reshape(rows, features)
    ids = expert_ids.reshape(rows, -1)
    route = route_weights.reshape(rows, -1)

    partial = jnp.dot(inputs, latent_down, preferred_element_type=jnp.float32).astype(jnp.bfloat16)
    latent = add(
        partial, *[shift(partial, "tensor", tensor_count, s) for s in range(1, tensor_count)]
    ).astype(jnp.bfloat16)

    weights = slot_weights(ids, route, expert_slot)
    slots = weights.shape[1]
    padded = -(-slots // LANES) * LANES
    payload = jnp.concatenate([latent, jnp.pad(weights, ((0, 0), (0, padded - slots)))], axis=1)

    near = jnp.concatenate(
        [payload] + [shift(payload, "expert", expert_axis, s * pair) for s in range(1, far)], axis=0
    )
    gathered = jnp.concatenate([near, swap(near)], axis=0) if pair == 2 else near
    mine = lax.dynamic_slice_in_dim(
        gathered[:, latent_width:], expert_index * local_count, local_count, axis=1
    ).astype(jnp.float32)
    mine = jnp.pad(mine, ((0, 0), (0, LANES - local_count)))
    mixed = experts(gathered[:, :latent_width], mine, gate_proj, up_proj, down_proj)

    if pair == 2:
        half = far * rows
        mixed = add(mixed[:half], swap(mixed[half:])).astype(jnp.bfloat16)
    block = latent_width // tensor_count

    def features_of(x, index, width):
        return lax.dynamic_slice_in_dim(x, index * width, width, axis=1)

    own = features_of(mixed, tensor_index, block)
    for s in range(1, tensor_count):
        away = features_of(mixed, (tensor_index + s) % tensor_count, block)
        own = add(own, shift(away, "tensor", tensor_count, s))
    own = own.astype(jnp.bfloat16).reshape(far, rows, block)
    total = add(
        own[0], *[shift(own[s], "expert", expert_axis, -s * pair) for s in range(1, far)]
    )
    norm = jnp.sum(route, axis=1, keepdims=True).astype(jnp.float32)
    mixed_rows = (total / norm).astype(jnp.bfloat16)

    result = inputs.astype(jnp.float32)
    for s in range(1, tensor_count):
        away = jnp.dot(
            mixed_rows,
            features_of(latent_up, (tensor_index + s) % tensor_count, features),
            preferred_element_type=jnp.float32,
        ).astype(jnp.bfloat16)
        result = result + shift(away, "tensor", tensor_count, s).astype(jnp.float32)
    result = result + jnp.dot(
        mixed_rows, features_of(latent_up, tensor_index, features), preferred_element_type=jnp.float32
    )
    return result.astype(jnp.bfloat16).reshape(steps, step_rows, features)


def solution(mesh):
    in_specs = (
        P(None, ("groups", "expert", "dp"), "tensor"),
        P(None, ("groups", "expert", "dp"), None),
        P(None, ("groups", "expert", "dp"), None),
        P(),
        P("tensor", None),
        P("expert", None, "tensor"),
        P("expert", None, "tensor"),
        P("expert", "tensor", None),
        P("tensor", None),
    )
    out_specs = P(None, ("groups", "expert", "dp"), "tensor")
    return jax.shard_map(shards, mesh=mesh, in_specs=in_specs, out_specs=out_specs, check_vma=False)
```

```python
import functools

import jax
import jax.numpy as jnp
from jax import lax
from jax.experimental import pallas as pl
from jax.experimental.pallas import tpu as pltpu
from jax.sharding import PartitionSpec as P

LANES = 128
VMEM_LIMIT = 24 * 1024 * 1024
CHEAP = pl.CostEstimate(flops=1, bytes_accessed=1, transcendentals=0)


def whole(count):
    return [pl.BlockSpec(memory_space=pltpu.VMEM)] * count


def call(kernel, out_shape, *operands):
    shapes = [jax.ShapeDtypeStruct(shape, dtype) for shape, dtype in out_shape]
    return pl.pallas_call(
        kernel,
        in_specs=whole(len(operands)),
        out_specs=whole(len(shapes)),
        out_shape=shapes,
        compiler_params=pltpu.CompilerParams(vmem_limit_bytes=VMEM_LIMIT),
        cost_estimate=CHEAP,
    )(*operands)


def fetch_kernel(mark_ref, *refs):
    count = len(refs) // 2
    sems = refs[-1]
    copies = [pltpu.make_async_copy(refs[i], refs[count + i], sems.at[i]) for i in range(count)]
    for copy in copies:
        copy.start()
    for copy in copies:
        copy.wait()


def fetch(mark, *arrays):
    held = [pltpu.with_memory_space_constraint(a, pltpu.HBM) for a in arrays]
    return pl.pallas_call(
        fetch_kernel,
        in_specs=[pl.BlockSpec(memory_space=pl.ANY)]
        + [pl.BlockSpec(memory_space=pltpu.HBM)] * len(arrays),
        out_specs=whole(len(arrays)),
        out_shape=[pltpu.VMEM(a.shape, a.dtype) for a in arrays],
        scratch_shapes=[pltpu.SemaphoreType.DMA((len(arrays),))],
        compiler_params=pltpu.CompilerParams(vmem_limit_bytes=1024 * 1024),
        cost_estimate=CHEAP,
    )(mark, *held)


def route_kernel(ids_ref, route_ref, slot_ref, weight_ref, norm_ref):
    steps, top_count, rows = ids_ref.shape
    slots, padded = slot_ref.shape[1], weight_ref.shape[1]
    every = lax.broadcasted_iota(jnp.int32, (slots, rows), 0)
    move = lax.broadcasted_iota(jnp.int32, (padded, slots), 0) == slot_ref[...]
    move = jnp.where(move, 1.0, 0.0).astype(jnp.bfloat16)
    for s in range(steps):
        ids, route = ids_ref[s], route_ref[s].astype(jnp.float32)
        by_expert = jnp.zeros((slots, rows), jnp.float32)
        for k in range(top_count):
            by_expert = by_expert + jnp.where(every == ids[k : k + 1], route[k : k + 1], 0.0)
        by_slot = jnp.dot(move, by_expert.astype(jnp.bfloat16), preferred_element_type=jnp.float32)
        at = pl.ds(s * rows, rows)
        weight_ref[at, :] = by_slot.T.astype(jnp.bfloat16)
        norm = jnp.broadcast_to(jnp.sum(route, axis=0, keepdims=True), (norm_ref.shape[1], rows))
        norm_ref[at, :] = norm.T


def expert_kernel(own_ref, pair_ref, gate_ref, up_ref, down_ref, own_out_ref, pair_out_ref):
    local_count, width = gate_ref.shape[0], gate_ref.shape[1]
    both = jnp.concatenate([own_ref[...], pair_ref[...]], axis=0)
    rows, weights = both[:, :width], both[:, width:].astype(jnp.float32)
    lanes = lax.broadcasted_iota(jnp.int32, weights.shape, 1)
    first = lax.axis_index("expert") * local_count
    total = None
    for j in range(local_count):
        gate_act = jnp.dot(rows, gate_ref[j], preferred_element_type=jnp.float32)
        up_act = jnp.dot(rows, up_ref[j], preferred_element_type=jnp.float32)
        weight = jnp.sum(jnp.where(lanes == first + j, weights, 0.0), axis=1, keepdims=True)
        hidden = (gate_act / (1.0 + jnp.exp(-gate_act)) * up_act * weight).astype(jnp.bfloat16)
        term = jnp.dot(hidden, down_ref[j], preferred_element_type=jnp.float32)
        total = term if total is None else total + term
    total = total.astype(jnp.bfloat16)
    half = own_out_ref.shape[0]
    own_out_ref[...] = total[:half]
    pair_out_ref[...] = total[half:]


def fold_kernel(tensor_count, *refs):
    terms, outs = refs[:-tensor_count], refs[-tensor_count:]
    me = lax.axis_index("tensor")
    width = outs[0].shape[1]
    for s, out in enumerate(outs):
        at = pl.multiple_of(lax.rem(me + s, tensor_count) * width, width)
        total = terms[0][:, pl.ds(at, width)].astype(jnp.float32)
        for term in terms[1:]:
            total = total + term[:, pl.ds(at, width)].astype(jnp.float32)
        out[...] = total.astype(out.dtype)


def away_kernel(tensor_count, norm_ref, up_ref, *refs):
    pieces, mixed_ref, outs = refs[:-tensor_count], refs[-tensor_count], refs[1 - tensor_count :]
    total = pieces[0][...].astype(jnp.float32)
    for piece in pieces[1:]:
        total = total + piece[...].astype(jnp.float32)
    mixed = (total / norm_ref[:, :1]).astype(jnp.bfloat16)
    mixed_ref[...] = mixed
    me = lax.axis_index("tensor")
    for s, out in enumerate(outs):
        width = out.shape[1]
        at = pl.multiple_of(lax.rem(me + s + 1, tensor_count) * width, width)
        out[...] = jnp.dot(
            mixed, up_ref[:, pl.ds(at, width)], preferred_element_type=jnp.float32
        ).astype(out.dtype)


def held_kernel(up_ref, mixed_ref, inputs_ref, held_ref):
    width = held_ref.shape[1]
    at = pl.multiple_of(lax.axis_index("tensor") * width, width)
    held_ref[...] = inputs_ref[...].astype(jnp.float32) + jnp.dot(
        mixed_ref[...], up_ref[:, pl.ds(at, width)], preferred_element_type=jnp.float32
    )


def add(*terms):
    return functools.reduce(jnp.add, [t.astype(jnp.float32) for t in terms])


def shards(
    tokens,
    expert_ids,
    route_weights,
    expert_slot,
    latent_down,
    gate_proj,
    up_proj,
    down_proj,
    latent_up,
):
    steps, step_rows, features = tokens.shape
    rows = steps * step_rows
    latent_width = latent_down.shape[1]
    tensor_count = lax.axis_size("tensor")
    expert_axis = lax.axis_size("expert")
    pair = 2 if expert_axis % 2 == 0 else 1
    far = expert_axis // pair
    block = latent_width // tensor_count

    def across(x, s):
        return lax.ppermute(
            x, "tensor", [(i, (i + s) % tensor_count) for i in range(tensor_count)]
        )

    def swap(x):
        return lax.ppermute(x, "expert", [(i, i ^ 1) for i in range(expert_axis)])

    def far_swap(x, s, back=False):
        if far & (far - 1) == 0:
            return lax.ppermute(x, "expert", [(i, i ^ (s * pair)) for i in range(expert_axis)])
        by = (-s if back else s) * pair
        return lax.ppermute(x, "expert", [(i, (i + by) % expert_axis) for i in range(expert_axis)])

    inputs = tokens.reshape(rows, features)
    slots = expert_slot.shape[0]
    weights, norm = call(
        route_kernel,
        [((rows, -(-slots // LANES) * LANES), jnp.bfloat16), ((rows, LANES), jnp.float32)],
        expert_ids.transpose(0, 2, 1),
        route_weights.transpose(0, 2, 1),
        expert_slot.reshape(1, slots),
    )
    partial = jnp.dot(inputs, latent_down, preferred_element_type=jnp.float32).astype(jnp.bfloat16)
    latent = add(partial, *[across(partial, s) for s in range(1, tensor_count)])
    (gate_proj,) = fetch(partial, gate_proj)
    latent, weights, gate_proj = lax.optimization_barrier((latent, weights, gate_proj))
    payload = jnp.concatenate([latent.astype(jnp.bfloat16), weights], axis=1)
    blocks = [payload] + [far_swap(payload, s) for s in range(1, far)]
    up_proj, down_proj = fetch(payload, up_proj, down_proj)
    *blocks, up_proj, down_proj = lax.optimization_barrier((*blocks, up_proj, down_proj))

    def apply(own, other):
        shape = ((own.shape[0], latent_width), jnp.bfloat16)
        return call(expert_kernel, [shape] * 2, own, other, gate_proj, up_proj, down_proj)

    def fold(*terms):
        shape = ((terms[0].shape[0], block), jnp.bfloat16)
        return call(functools.partial(fold_kernel, tensor_count), [shape] * tensor_count, *terms)

    def halves(own):
        return (own, swap(own)) if pair == 2 else jnp.split(own, 2, axis=0)

    def join(own, other):
        return fold(own, swap(other)) if pair == 2 else fold(jnp.concatenate([own, other], axis=0))

    cut = far // 2
    pieces = []
    for part in (blocks[cut:], blocks[:cut]) if cut else (blocks,):
        own = jnp.concatenate(part, axis=0)
        held, *away = join(*apply(*halves(own)))
        arrived = [across(x, s + 1) for s, x in enumerate(away)]
        sums = add(held, *arrived).astype(jnp.bfloat16)
        pieces = [sums[i : i + rows] for i in range(0, sums.shape[0], rows)] + pieces
    (latent_up,) = fetch(pieces[-1], latent_up)
    pieces = [pieces[0]] + [far_swap(pieces[s], s, back=True) for s in range(1, far)]

    mixed_rows, *away = call(
        functools.partial(away_kernel, tensor_count),
        [((rows, block), jnp.bfloat16)] + [((rows, features), jnp.bfloat16)] * (tensor_count - 1),
        norm,
        latent_up,
        *pieces,
    )
    arrived = [across(x, s + 1) for s, x in enumerate(away)]
    (held,) = call(
        held_kernel, [((rows, features), jnp.float32)], latent_up, mixed_rows, inputs
    )
    return add(held, *arrived).astype(jnp.bfloat16).reshape(steps, step_rows, features)


def solution(mesh):
    in_specs = (
        P(None, ("groups", "expert", "dp"), "tensor"),
        P(None, ("groups", "expert", "dp"), None),
        P(None, ("groups", "expert", "dp"), None),
        P(),
        P("tensor", None),
        P("expert", None, "tensor"),
        P("expert", None, "tensor"),
        P("expert", "tensor", None),
        P("tensor", None),
    )
    out_specs = P(None, ("groups", "expert", "dp"), "tensor")
    return jax.shard_map(shards, mesh=mesh, in_specs=in_specs, out_specs=out_specs, check_vma=False)
```

```python
import functools

import jax
import jax.numpy as jnp
from jax import lax
from jax.experimental import pallas as pl
from jax.experimental.pallas import tpu as pltpu
from jax.sharding import PartitionSpec as P

LANES = 128
VMEM_LIMIT = 24 * 1024 * 1024
CHEAP = pl.CostEstimate(flops=1, bytes_accessed=1, transcendentals=0)


def whole(count):
    return [pl.BlockSpec(memory_space=pltpu.VMEM)] * count


def call(kernel, out_shape, *operands):
    shapes = [jax.ShapeDtypeStruct(shape, dtype) for shape, dtype in out_shape]
    return pl.pallas_call(
        kernel,
        in_specs=whole(len(operands)),
        out_specs=whole(len(shapes)),
        out_shape=shapes,
        compiler_params=pltpu.CompilerParams(vmem_limit_bytes=VMEM_LIMIT),
        cost_estimate=CHEAP,
    )(*operands)


def fetch_kernel(mark_ref, *refs):
    count = len(refs) // 2
    sems = refs[-1]
    copies = [pltpu.make_async_copy(refs[i], refs[count + i], sems.at[i]) for i in range(count)]
    for copy in copies:
        copy.start()
    for copy in copies:
        copy.wait()


def fetch(mark, *arrays):
    held = [pltpu.with_memory_space_constraint(a, pltpu.HBM) for a in arrays]
    return pl.pallas_call(
        fetch_kernel,
        in_specs=[pl.BlockSpec(memory_space=pl.ANY)]
        + [pl.BlockSpec(memory_space=pltpu.HBM)] * len(arrays),
        out_specs=whole(len(arrays)),
        out_shape=[pltpu.VMEM(a.shape, a.dtype) for a in arrays],
        scratch_shapes=[pltpu.SemaphoreType.DMA((len(arrays),))],
        compiler_params=pltpu.CompilerParams(vmem_limit_bytes=1024 * 1024),
        cost_estimate=CHEAP,
    )(mark, *held)


def route_kernel(ids_ref, route_ref, slot_ref, packed_ref, norm_ref):
    steps, top_count, rows = ids_ref.shape
    slots, group = slot_ref.shape[1], packed_ref.shape[0]
    every = lax.broadcasted_iota(jnp.int32, (slots, rows), 0)
    move = lax.broadcasted_iota(jnp.int32, (LANES, slots), 0) == slot_ref[...]
    move = jnp.where(move, 1.0, 0.0).astype(jnp.bfloat16)
    packed = None
    for s in range(steps):
        ids, route = ids_ref[s], route_ref[s].astype(jnp.float32)
        by_expert = jnp.zeros((slots, rows), jnp.float32)
        for k in range(top_count):
            by_expert = by_expert + jnp.where(every == ids[k : k + 1], route[k : k + 1], 0.0)
        by_slot = jnp.dot(move, by_expert.astype(jnp.bfloat16), preferred_element_type=jnp.float32).T
        for g in range(rows // group):
            at = (s * rows // group + g) * slots
            part = by_slot[g * group : (g + 1) * group]
            part = pltpu.roll(part, at, 1) if at else part
            packed = part if packed is None else packed + part
        norm = jnp.broadcast_to(jnp.sum(route, axis=0, keepdims=True), (norm_ref.shape[1], rows))
        norm_ref[pl.ds(s * rows, rows), :] = norm.T
    packed_ref[...] = packed.astype(packed_ref.dtype)


def pack_kernel(*refs):
    *terms, packed_ref, out_ref = refs
    rows, width = terms[0].shape
    for c in range(width // LANES):
        at = slice(c * LANES, (c + 1) * LANES)
        total = terms[0][:, at].astype(jnp.float32)
        for term in terms[1:]:
            total = total + term[:, at].astype(jnp.float32)
        out_ref[c * rows : (c + 1) * rows, :] = total.astype(out_ref.dtype)
    out_ref[width // LANES * rows :, :] = packed_ref[...]


def expert_kernel(rows, slots, own_ref, pair_ref, gate_ref, up_ref, down_ref, own_out_ref, pair_out_ref):
    local_count, width = gate_ref.shape[0], gate_ref.shape[1]
    columns, group = width // LANES, rows * slots // LANES
    size = columns * rows + group
    latent, packed = [], []
    for ref in (own_ref, pair_ref):
        for b in range(0, ref.shape[0], size):
            parts = [ref[b + c * rows : b + (c + 1) * rows, :] for c in range(columns)]
            latent.append(jnp.concatenate(parts, axis=1))
            packed.append(ref[b + columns * rows : b + size, :])
    both, packed = jnp.concatenate(latent, axis=0), jnp.concatenate(packed, axis=0)
    first = lax.axis_index("expert") * local_count
    lane = lax.broadcasted_iota(jnp.int32, (LANES, LANES), 0)
    column = lax.broadcasted_iota(jnp.int32, (LANES, LANES), 1)
    spread = []
    for g in range(LANES // slots):
        take = jnp.where(lane == column + (first + g * slots), 1.0, 0.0).astype(jnp.bfloat16)
        spread.append(jnp.dot(packed, take, preferred_element_type=jnp.float32))
    weights = jnp.concatenate(
        [part[b : b + group] for b in range(0, packed.shape[0], group) for part in spread], axis=0
    )
    hidden = []
    for j in range(local_count):
        gate_act = jnp.dot(both, gate_ref[j], preferred_element_type=jnp.float32)
        up_act = jnp.dot(both, up_ref[j], preferred_element_type=jnp.float32)
        silu = gate_act / (1.0 + jnp.exp(-gate_act))
        hidden.append((silu * up_act * weights[:, j : j + 1]).astype(jnp.bfloat16))
    hidden = jnp.concatenate(hidden, axis=1)
    down = down_ref[...].reshape(hidden.shape[1], width)
    total = jnp.dot(hidden, down, preferred_element_type=jnp.float32).astype(jnp.bfloat16)
    half_rows = own_out_ref.shape[0]
    own_out_ref[...] = total[:half_rows]
    pair_out_ref[...] = total[half_rows:]


def fold_kernel(tensor_count, *refs):
    terms, outs = refs[:-tensor_count], refs[-tensor_count:]
    me = lax.axis_index("tensor")
    width = outs[0].shape[1]
    for s, out in enumerate(outs):
        at = pl.multiple_of(lax.rem(me + s, tensor_count) * width, width)
        total = terms[0][:, pl.ds(at, width)].astype(jnp.float32)
        for term in terms[1:]:
            total = total + term[:, pl.ds(at, width)].astype(jnp.float32)
        out[...] = total.astype(out.dtype)


def away_kernel(tensor_count, norm_ref, up_ref, *refs):
    pieces, mixed_ref, outs = refs[:-tensor_count], refs[-tensor_count], refs[1 - tensor_count :]
    total = pieces[0][...].astype(jnp.float32)
    for piece in pieces[1:]:
        total = total + piece[...].astype(jnp.float32)
    mixed = (total / norm_ref[:, :1]).astype(jnp.bfloat16)
    mixed_ref[...] = mixed
    me = lax.axis_index("tensor")
    for s, out in enumerate(outs):
        width = out.shape[1]
        at = pl.multiple_of(lax.rem(me + s + 1, tensor_count) * width, width)
        out[...] = jnp.dot(
            mixed, up_ref[:, pl.ds(at, width)], preferred_element_type=jnp.float32
        ).astype(out.dtype)


def held_kernel(up_ref, mixed_ref, inputs_ref, held_ref):
    width = held_ref.shape[1]
    at = pl.multiple_of(lax.axis_index("tensor") * width, width)
    held_ref[...] = inputs_ref[...].astype(jnp.float32) + jnp.dot(
        mixed_ref[...], up_ref[:, pl.ds(at, width)], preferred_element_type=jnp.float32
    )


def add(*terms):
    return functools.reduce(jnp.add, [t.astype(jnp.float32) for t in terms])


def shards(
    tokens,
    expert_ids,
    route_weights,
    expert_slot,
    latent_down,
    gate_proj,
    up_proj,
    down_proj,
    latent_up,
):
    steps, step_rows, features = tokens.shape
    rows = steps * step_rows
    latent_width = latent_down.shape[1]
    tensor_count = lax.axis_size("tensor")
    expert_axis = lax.axis_size("expert")
    pair = 2 if expert_axis % 2 == 0 else 1
    far = expert_axis // pair
    block = latent_width // tensor_count

    def across(x, s):
        return lax.ppermute(
            x, "tensor", [(i, (i + s) % tensor_count) for i in range(tensor_count)]
        )

    def swap(x):
        return lax.ppermute(x, "expert", [(i, i ^ 1) for i in range(expert_axis)])

    def far_swap(x, s, back=False):
        if far & (far - 1) == 0:
            return lax.ppermute(x, "expert", [(i, i ^ (s * pair)) for i in range(expert_axis)])
        by = (-s if back else s) * pair
        return lax.ppermute(x, "expert", [(i, (i + by) % expert_axis) for i in range(expert_axis)])

    inputs = tokens.reshape(rows, features)
    slots = expert_slot.shape[0]
    packed, norm = call(
        route_kernel,
        [((rows * slots // LANES, LANES), jnp.bfloat16), ((rows, LANES), jnp.float32)],
        expert_ids.transpose(0, 2, 1),
        route_weights.transpose(0, 2, 1),
        expert_slot.reshape(1, slots),
    )
    partial = jnp.dot(inputs, latent_down, preferred_element_type=jnp.float32).astype(jnp.bfloat16)
    terms = [partial] + [across(partial, s) for s in range(1, tensor_count)]
    (gate_proj,) = fetch(partial, gate_proj)
    terms, packed, gate_proj = lax.optimization_barrier((terms, packed, gate_proj))
    size = rows * latent_width // LANES + packed.shape[0]
    (payload,) = call(pack_kernel, [((size, LANES), jnp.bfloat16)], *terms, packed)
    blocks = [payload] + [far_swap(payload, s) for s in range(1, far)]
    up_proj, down_proj = fetch(payload, up_proj, down_proj)

    def apply(own, other):
        shape = ((own.shape[0] // size * rows, latent_width), jnp.bfloat16)
        kernel = functools.partial(expert_kernel, rows, slots)
        return call(kernel, [shape] * 2, own, other, gate_proj, up_proj, down_proj)

    def fold(*terms):
        shape = ((terms[0].shape[0], block), jnp.bfloat16)
        return call(functools.partial(fold_kernel, tensor_count), [shape] * tensor_count, *terms)

    def halves(own):
        return (own, swap(own)) if pair == 2 else jnp.split(own, 2, axis=0)

    def join(own, other):
        return fold(own, swap(other)) if pair == 2 else fold(jnp.concatenate([own, other], axis=0))

    def spread(held, *away):
        arrived = [across(x, s + 1) for s, x in enumerate(away)]
        sums = add(held, *arrived).astype(jnp.bfloat16)
        return [sums[i : i + rows] for i in range(0, sums.shape[0], rows)]

    def run(part):
        return join(*apply(*halves(jnp.concatenate(part, axis=0))))

    cut = max(far // 2, 1)
    first = run(blocks[:1])
    *first, up_proj, down_proj, blocks[1:] = lax.optimization_barrier(
        (*first, up_proj, down_proj, blocks[1:])
    )
    pieces = spread(*first)
    if far > cut:
        last = run(blocks[cut:])
        if cut > 1:
            *last, blocks[1] = lax.optimization_barrier((*last, blocks[1]))
            middle = run(blocks[1:cut])
            last = spread(*last)
            pieces += spread(*middle) + last
        else:
            pieces += spread(*last)
    (latent_up,) = fetch(pieces[-1], latent_up)
    pieces = [pieces[0]] + [far_swap(pieces[s], s, back=True) for s in range(1, far)]

    mixed_rows, *away = call(
        functools.partial(away_kernel, tensor_count),
        [((rows, block), jnp.bfloat16)] + [((rows, features), jnp.bfloat16)] * (tensor_count - 1),
        norm,
        latent_up,
        *pieces,
    )
    arrived = [across(x, s + 1) for s, x in enumerate(away)]
    (held,) = call(
        held_kernel, [((rows, features), jnp.float32)], latent_up, mixed_rows, inputs
    )
    return add(held, *arrived).astype(jnp.bfloat16).reshape(steps, step_rows, features)


def solution(mesh):
    in_specs = (
        P(None, ("groups", "expert", "dp"), "tensor"),
        P(None, ("groups", "expert", "dp"), None),
        P(None, ("groups", "expert", "dp"), None),
        P(),
        P("tensor", None),
        P("expert", None, "tensor"),
        P("expert", None, "tensor"),
        P("expert", "tensor", None),
        P("tensor", None),
    )
    out_specs = P(None, ("groups", "expert", "dp"), "tensor")
    return jax.shard_map(shards, mesh=mesh, in_specs=in_specs, out_specs=out_specs, check_vma=False)
```

```python
import functools

import jax
import jax.numpy as jnp
from jax import lax
from jax.experimental import pallas as pl
from jax.experimental.pallas import tpu as pltpu
from jax.sharding import PartitionSpec as P

LANES = 128
VMEM_LIMIT = 24 * 1024 * 1024
CHEAP = pl.CostEstimate(flops=1, bytes_accessed=1, transcendentals=0)


def whole(count):
    return [pl.BlockSpec(memory_space=pltpu.VMEM)] * count


def call(kernel, out_shape, *operands):
    shapes = [jax.ShapeDtypeStruct(shape, dtype) for shape, dtype in out_shape]
    return pl.pallas_call(
        kernel,
        in_specs=whole(len(operands)),
        out_specs=whole(len(shapes)),
        out_shape=shapes,
        compiler_params=pltpu.CompilerParams(vmem_limit_bytes=VMEM_LIMIT),
        cost_estimate=CHEAP,
    )(*operands)


def fetch_kernel(mark_ref, *refs):
    count = len(refs) // 2
    sems = refs[-1]
    copies = [pltpu.make_async_copy(refs[i], refs[count + i], sems.at[i]) for i in range(count)]
    for copy in copies:
        copy.start()
    for copy in copies:
        copy.wait()


def fetch(mark, *arrays):
    held = [pltpu.with_memory_space_constraint(a, pltpu.HBM) for a in arrays]
    return pl.pallas_call(
        fetch_kernel,
        in_specs=[pl.BlockSpec(memory_space=pl.ANY)]
        + [pl.BlockSpec(memory_space=pltpu.HBM)] * len(arrays),
        out_specs=whole(len(arrays)),
        out_shape=[pltpu.VMEM(a.shape, a.dtype) for a in arrays],
        scratch_shapes=[pltpu.SemaphoreType.DMA((len(arrays),))],
        compiler_params=pltpu.CompilerParams(vmem_limit_bytes=1024 * 1024),
        cost_estimate=CHEAP,
    )(mark, *held)


def route_kernel(ids_ref, route_ref, slot_ref, packed_ref, norm_ref):
    steps, top_count, rows = ids_ref.shape
    slots, group = slot_ref.shape[1], packed_ref.shape[0]
    every = lax.broadcasted_iota(jnp.int32, (slots, rows), 0)
    move = lax.broadcasted_iota(jnp.int32, (LANES, slots), 0) == slot_ref[...]
    move = jnp.where(move, 1.0, 0.0).astype(jnp.bfloat16)
    packed = None
    for s in range(steps):
        ids, route = ids_ref[s], route_ref[s].astype(jnp.float32)
        by_expert = jnp.zeros((slots, rows), jnp.float32)
        for k in range(top_count):
            by_expert = by_expert + jnp.where(every == ids[k : k + 1], route[k : k + 1], 0.0)
        by_slot = jnp.dot(move, by_expert.astype(jnp.bfloat16), preferred_element_type=jnp.float32).T
        for g in range(rows // group):
            at = (s * rows // group + g) * slots
            part = by_slot[g * group : (g + 1) * group]
            part = pltpu.roll(part, at, 1) if at else part
            packed = part if packed is None else packed + part
        norm = jnp.broadcast_to(jnp.sum(route, axis=0, keepdims=True), (norm_ref.shape[1], rows))
        norm_ref[pl.ds(s * rows, rows), :] = norm.T
    packed_ref[...] = packed.astype(packed_ref.dtype)


def pack_kernel(*refs):
    *terms, packed_ref, out_ref = refs
    rows, width = terms[0].shape
    for c in range(width // LANES):
        at = slice(c * LANES, (c + 1) * LANES)
        total = terms[0][:, at].astype(jnp.float32)
        for term in terms[1:]:
            total = total + term[:, at].astype(jnp.float32)
        out_ref[c * rows : (c + 1) * rows, :] = total.astype(out_ref.dtype)
    out_ref[width // LANES * rows :, :] = packed_ref[...]


def expert_kernel(rows, slots, gate_ref, up_ref, down_ref, *refs):
    payloads, outs = refs[: len(refs) // 2], refs[len(refs) // 2 :]
    local_count, width = gate_ref.shape[0], gate_ref.shape[1]
    columns, group = width // LANES, rows * slots // LANES
    size = columns * rows + group
    latent, packed = [], []
    for ref in payloads:
        for b in range(0, ref.shape[0], size):
            parts = [ref[b + c * rows : b + (c + 1) * rows, :] for c in range(columns)]
            latent.append(jnp.concatenate(parts, axis=1))
            packed.append(ref[b + columns * rows : b + size, :])
    both, packed = jnp.concatenate(latent, axis=0), jnp.concatenate(packed, axis=0)
    first = lax.axis_index("expert") * local_count
    lane = lax.broadcasted_iota(jnp.int32, (LANES, LANES), 0)
    column = lax.broadcasted_iota(jnp.int32, (LANES, LANES), 1)
    spread = []
    for g in range(LANES // slots):
        take = jnp.where(lane == column + (first + g * slots), 1.0, 0.0).astype(jnp.bfloat16)
        spread.append(jnp.dot(packed, take, preferred_element_type=jnp.float32))
    weights = jnp.concatenate(
        [part[b : b + group] for b in range(0, packed.shape[0], group) for part in spread], axis=0
    )
    hidden = []
    for j in range(local_count):
        gate_act = jnp.dot(both, gate_ref[j], preferred_element_type=jnp.float32)
        up_act = jnp.dot(both, up_ref[j], preferred_element_type=jnp.float32)
        silu = gate_act / (1.0 + jnp.exp(-gate_act))
        hidden.append((silu * up_act * weights[:, j : j + 1]).astype(jnp.bfloat16))
    hidden = jnp.concatenate(hidden, axis=1)
    down = down_ref[...].reshape(hidden.shape[1], width)
    total = jnp.dot(hidden, down, preferred_element_type=jnp.float32).astype(jnp.bfloat16)
    at = 0
    for out in outs:
        out[...] = total[at : at + out.shape[0]]
        at += out.shape[0]


def fold_kernel(tensor_count, *refs):
    terms, outs = refs[:-tensor_count], refs[-tensor_count:]
    me = lax.axis_index("tensor")
    width = outs[0].shape[1]
    for s, out in enumerate(outs):
        at = pl.multiple_of(lax.rem(me + s, tensor_count) * width, width)
        total = terms[0][:, pl.ds(at, width)].astype(jnp.float32)
        for term in terms[1:]:
            total = total + term[:, pl.ds(at, width)].astype(jnp.float32)
        out[...] = total.astype(out.dtype)


def away_kernel(tensor_count, norm_ref, up_ref, *refs):
    pieces, mixed_ref, outs = refs[:-tensor_count], refs[-tensor_count], refs[1 - tensor_count :]
    total = pieces[0][...].astype(jnp.float32)
    for piece in pieces[1:]:
        total = total + piece[...].astype(jnp.float32)
    mixed = (total / norm_ref[:, :1]).astype(jnp.bfloat16)
    mixed_ref[...] = mixed
    me = lax.axis_index("tensor")
    for s, out in enumerate(outs):
        width = out.shape[1]
        at = pl.multiple_of(lax.rem(me + s + 1, tensor_count) * width, width)
        out[...] = jnp.dot(
            mixed, up_ref[:, pl.ds(at, width)], preferred_element_type=jnp.float32
        ).astype(out.dtype)


def held_kernel(up_ref, mixed_ref, inputs_ref, held_ref):
    width = held_ref.shape[1]
    at = pl.multiple_of(lax.axis_index("tensor") * width, width)
    held_ref[...] = inputs_ref[...].astype(jnp.float32) + jnp.dot(
        mixed_ref[...], up_ref[:, pl.ds(at, width)], preferred_element_type=jnp.float32
    )


def add(*terms):
    return functools.reduce(jnp.add, [t.astype(jnp.float32) for t in terms])


def shards(
    tokens,
    expert_ids,
    route_weights,
    expert_slot,
    latent_down,
    gate_proj,
    up_proj,
    down_proj,
    latent_up,
):
    steps, step_rows, features = tokens.shape
    rows = steps * step_rows
    latent_width = latent_down.shape[1]
    tensor_count = lax.axis_size("tensor")
    expert_axis = lax.axis_size("expert")
    pair = 2 if expert_axis % 2 == 0 else 1
    far = expert_axis // pair
    block = latent_width // tensor_count

    def across(x, s):
        return lax.ppermute(
            x, "tensor", [(i, (i + s) % tensor_count) for i in range(tensor_count)]
        )

    def swap(x):
        return lax.ppermute(x, "expert", [(i, i ^ 1) for i in range(expert_axis)])

    def far_swap(x, s, back=False):
        if far & (far - 1) == 0:
            return lax.ppermute(x, "expert", [(i, i ^ (s * pair)) for i in range(expert_axis)])
        by = (-s if back else s) * pair
        return lax.ppermute(x, "expert", [(i, (i + by) % expert_axis) for i in range(expert_axis)])

    inputs = tokens.reshape(rows, features)
    slots = expert_slot.shape[0]
    packed, norm = call(
        route_kernel,
        [((rows * slots // LANES, LANES), jnp.bfloat16), ((rows, LANES), jnp.float32)],
        expert_ids.transpose(0, 2, 1),
        route_weights.transpose(0, 2, 1),
        expert_slot.reshape(1, slots),
    )
    partial = jnp.dot(inputs, latent_down, preferred_element_type=jnp.float32).astype(jnp.bfloat16)
    terms = [partial] + [across(partial, s) for s in range(1, tensor_count)]
    (gate_proj,) = fetch(partial, gate_proj)
    terms, packed, gate_proj = lax.optimization_barrier((terms, packed, gate_proj))
    size = rows * latent_width // LANES + packed.shape[0]
    (payload,) = call(pack_kernel, [((size, LANES), jnp.bfloat16)], *terms, packed)
    blocks = [payload] + [far_swap(payload, s) for s in range(1, far)]
    up_proj, down_proj = fetch(payload, up_proj, down_proj)

    def apply(*payloads):
        shapes = [((x.shape[0] // size * rows, latent_width), jnp.bfloat16) for x in payloads]
        kernel = functools.partial(expert_kernel, rows, slots)
        return call(kernel, shapes, gate_proj, up_proj, down_proj, *payloads)

    def fold(*terms):
        shape = ((terms[0].shape[0], block), jnp.bfloat16)
        return call(functools.partial(fold_kernel, tensor_count), [shape] * tensor_count, *terms)

    def halves(own):
        return (own, swap(own)) if pair == 2 else jnp.split(own, 2, axis=0)

    def join(own, other):
        return fold(own, swap(other)) if pair == 2 else fold(jnp.concatenate([own, other], axis=0))

    def spread(held, *away):
        arrived = [across(x, s + 1) for s, x in enumerate(away)]
        sums = add(held, *arrived).astype(jnp.bfloat16)
        return [sums[i : i + rows] for i in range(0, sums.shape[0], rows)]

    def run(part):
        return join(*apply(*halves(jnp.concatenate(part, axis=0))))

    cut = max(far // 2, 1)
    first = run(blocks[:1])
    *first, up_proj, down_proj, blocks[1:] = lax.optimization_barrier(
        (*first, up_proj, down_proj, blocks[1:])
    )
    pieces = spread(*first)
    if far > cut:
        own, other = halves(jnp.concatenate(blocks[cut:], axis=0))
        last = [*apply(own), *apply(other)]
        if cut > 1:
            middle = halves(jnp.concatenate(blocks[1:cut], axis=0))
            last, middle = lax.optimization_barrier((last, middle))
            middle = apply(*middle)
            last = join(*last)
            last, middle = lax.optimization_barrier((last, middle))
            pieces += spread(*join(*middle)) + spread(*last)
        else:
            pieces += spread(*join(*last))
    (latent_up,) = fetch(pieces[-1], latent_up)
    pieces = [pieces[0]] + [far_swap(pieces[s], s, back=True) for s in range(1, far)]

    mixed_rows, *away = call(
        functools.partial(away_kernel, tensor_count),
        [((rows, block), jnp.bfloat16)] + [((rows, features), jnp.bfloat16)] * (tensor_count - 1),
        norm,
        latent_up,
        *pieces,
    )
    arrived = [across(x, s + 1) for s, x in enumerate(away)]
    (held,) = call(
        held_kernel, [((rows, features), jnp.float32)], latent_up, mixed_rows, inputs
    )
    return add(held, *arrived).astype(jnp.bfloat16).reshape(steps, step_rows, features)


def solution(mesh):
    in_specs = (
        P(None, ("groups", "expert", "dp"), "tensor"),
        P(None, ("groups", "expert", "dp"), None),
        P(None, ("groups", "expert", "dp"), None),
        P(),
        P("tensor", None),
        P("expert", None, "tensor"),
        P("expert", None, "tensor"),
        P("expert", "tensor", None),
        P("tensor", None),
    )
    out_specs = P(None, ("groups", "expert", "dp"), "tensor")
    return jax.shard_map(shards, mesh=mesh, in_specs=in_specs, out_specs=out_specs, check_vma=False)
```
